256 devices in a mesh: term: 8 (over y, x_lo), sector: 32 (over x_hi, z, core).
Axes of the slice: x: 4 (x_hi: 2, x_lo: 2; x = x_hi * 2 + x_lo), y: 4, z: 8, core: 2. Of those that a mesh axis runs over, the one named last changes fastest.
Arguments:
- psi: bfloat16 [32, 512, 512], P('sector'), may hold values from -6 to 6
- left_blocks: bfloat16 [64, 32, 512, 512], P('term', 'sector'), may hold values from -0.09375 to 0.09375
- right_ops: bfloat16 [64, 512, 512], P('term'), may hold values from -0.25 to 0.25
- sector_rows: int32 [32], replicated, may hold values from 128 to 512, as said below
- connect: int32 [64, 32], replicated, may hold values from 0 to 31, each once within a row
- term_order: int32 [64], replicated, may hold values from 0 to 63, each once
- sector_at: int32 [32], replicated, may hold values from 0 to 31, each once
Outputs:
- sigma: float32 [32, 512, 512], P('sector', None, 'term')
The draws below stay inside these ranges and needn't reach their ends.
Inputs may be any that keep to these rules, and one draw needn't show every extreme that they name: `sector_rows`: live rows of each sector; rows from this count up to 512 of a block are padding. Some sector has exactly 512 and some exactly 128. `connect`: each row is a permutation of the sector ids. `term_order`: A permutation of the terms. `sector_at`: A permutation of the sector ids.
All inputs are finite; a program needn't handle non-finite values.
Results may differ from the reference program's by a relative error of at most 0.0003.
Values may be sent and summed in bfloat16 or wider, within the bound.
No kernel may reach another device: no remote copies, remote signals or barrier semaphores. Data moves between devices by JAX's collectives and lax.ppermute only.
A program may use at most 128 MiB of HBM per device.

```python
import jax
import jax.numpy as jnp
from jax import lax

BLK = 512
COLS = 512
TERMS = 64
SECTORS = 32


def draw_sector_rows(key, part):
    key = jax.random.fold_in(key, 11)
    key_first, key_second = jax.random.split(key, 2)
    counts = jax.random.randint(key_first, (SECTORS,), BLK // 4, BLK + 1)
    chosen = jax.random.permutation(key_second, SECTORS)
    counts = counts.at[chosen[0]].set(BLK)
    counts = counts.at[chosen[1]].set(BLK // 4)
    return counts.astype(jnp.int32)


def block_levels(key, extent, cuts, low, top_value):
    level, own = 1.0, jax.random.fold_in(key, 6)
    for dim, shards_of in cuts:
        heights = jnp.exp(jax.random.uniform(jax.random.fold_in(own, dim), (shards_of,), jnp.float32, low / len(cuts), top_value / len(cuts)))
        level = level * jnp.repeat(heights, extent[dim] // shards_of).reshape([-1 if axis == dim else 1 for axis in range(len(extent))])
    return level


def gaussian(stream_key, extent, spread, reach, cuts=(), held_as=jnp.bfloat16):
    values = jax.random.normal(stream_key, extent, jnp.float32) * spread
    if len(cuts) > 0:
        values = block_levels(stream_key, extent, cuts, -0.22, 0.18) * values
    return jnp.clip(values, min=-reach, max=reach).astype(held_as)


def setup_inputs(seed: int = 0) -> dict:
    seeds = jax.random.split(jax.random.key(seed), 8)
    psi = gaussian(seeds[0], (SECTORS, BLK, COLS), 1.0, 6.0, ((0, 32),))
    left_blocks = gaussian(seeds[1], (TERMS, SECTORS, BLK, BLK), (8 * BLK) ** -0.5, 0.09375, ((0, 8), (1, 32)))
    right_ops = gaussian(seeds[2], (TERMS, COLS, COLS), COLS ** -0.5, 0.25, ((0, 8),))
    sector_rows = draw_sector_rows(jax.random.fold_in(seeds[7], 71), 0)
    connect = jax.vmap(lambda own: jax.random.permutation(own, SECTORS))(jax.random.split(seeds[4], TERMS)).reshape((TERMS, SECTORS)).astype(jnp.int32)
    term_order = jax.random.permutation(seeds[5], TERMS).astype(jnp.int32)
    sector_at = jax.random.permutation(seeds[6], SECTORS).astype(jnp.int32)
    return {"psi": psi, "left_blocks": left_blocks, "right_ops": right_ops, "sector_rows": sector_rows, "connect": connect, "term_order": term_order, "sector_at": sector_at}


def reference(psi, left_blocks, right_ops, sector_rows, connect, term_order, sector_at):
    ids = jnp.arange(SECTORS, dtype=jnp.int32)
    position = jnp.sum(jnp.where(sector_at[None, :] == ids[:, None], ids[None, :], 0), axis=1).astype(jnp.int32)
    row_index = jnp.arange(BLK, dtype=jnp.int32)

    def per_target(place):
        target = sector_at[place]
        sources = connect[term_order, target]
        blocks = psi[position[sources]]
        live_rows = row_index[None, :] < sector_rows[sources][:, None]
        blocks = jnp.where(live_rows[:, :, None], blocks, jnp.zeros((), psi.dtype))
        lefts = left_blocks[:, place]
        inner_part = jnp.einsum("kab,kbc->kac", lefts.astype(jnp.float32), blocks.astype(jnp.float32), precision=lax.Precision.HIGHEST)
        outer_part = jnp.einsum("kac,kcd->kad", inner_part, right_ops.astype(jnp.float32), precision=lax.Precision.HIGHEST)
        summed = jnp.sum(outer_part, axis=0)
        return jnp.where((row_index < sector_rows[target])[:, None], summed, jnp.zeros((), summed.dtype))

    return lax.map(per_target, ids)
```

```python
import functools

import jax
import jax.numpy as jnp
from jax import lax
from jax.experimental import pallas as pl
from jax.experimental.pallas import tpu as pltpu
from jax.sharding import PartitionSpec as P

GROUPS = 8
SLOTS = 8
PLACES = 32
BLK = 512
PART = BLK // GROUPS


def place_permutation(f):
    return [(s, f(s)) for s in range(PLACES)]


def find_positions(sector_at, position):
    def put(p, carry):
        position[sector_at[p]] = p
        return carry

    lax.fori_loop(0, PLACES, put, 0)


def select_kernel(where, term_order, connect, sector_at, own, other, out, position, sem):
    find_positions(sector_at, position)
    place = where[1]
    core = lax.rem(place, 2)
    target = sector_at[place]

    def start(i, carry):
        p = position[connect[term_order[i], target]]
        half = lax.div(p, 2)
        mine = lax.rem(p, 2) == core
        dst = out.at[i]

        @pl.when(mine)
        def _():
            pltpu.make_async_copy(own.at[half], dst, sem).start()

        @pl.when(jnp.logical_not(mine))
        def _():
            pltpu.make_async_copy(other.at[half], dst, sem).start()

        return carry

    lax.fori_loop(0, GROUPS * SLOTS, start, 0)
    pltpu.make_async_copy(out, out, sem).wait()


def product_kernel(where, term_order, connect, sector_at, sector_rows, block, left, right, out, acc):
    k = pl.program_id(0)
    group, place = where[0], where[1]
    target = sector_at[place]
    source = connect[term_order[group * SLOTS + k], target]
    live = sector_rows[source]
    rows = lax.broadcasted_iota(jnp.int32, (BLK, BLK), 0)
    b = block[...].reshape(BLK, BLK)
    b = jnp.where(rows < live, b, jnp.zeros((), b.dtype))
    t = jnp.dot(b, right[0], preferred_element_type=jnp.float32)
    hi = t.astype(jnp.bfloat16)
    lo = (t - hi.astype(jnp.float32)).astype(jnp.bfloat16)
    l = left[0, 0]
    part = jnp.dot(l, hi, preferred_element_type=jnp.float32) + jnp.dot(
        l, lo, preferred_element_type=jnp.float32
    )

    @pl.when(k == 0)
    def _():
        acc[...] = part

    @pl.when(k > 0)
    def _():
        acc[...] += part

    @pl.when(k == SLOTS - 1)
    def _():
        total = jnp.where(rows < sector_rows[target], acc[...], 0.0)
        out[...] = total.T


def on_device(psi, left_blocks, right_ops, sector_rows, connect, term_order, sector_at):
    group = lax.axis_index("term")
    place = lax.axis_index("sector")
    where = jnp.stack([group, place]).astype(jnp.int32)
    smem = pl.BlockSpec(memory_space=pltpu.SMEM)
    hbm = pl.BlockSpec(memory_space=pl.ANY)

    part = lax.dynamic_slice_in_dim(psi[0], group * PART, PART)
    copies = jnp.broadcast_to(part[None], (PLACES // 2, PART, BLK))
    same_core = [[c + 2 * h for h in range(PLACES // 2)] for c in range(2)]
    own = lax.all_to_all(copies, "sector", 0, 0, axis_index_groups=same_core, tiled=True)
    other = lax.ppermute(own, "sector", place_permutation(lambda s: s ^ 1))
    chosen = pl.pallas_call(
        select_kernel,
        out_shape=jax.ShapeDtypeStruct((GROUPS * SLOTS, PART, BLK), psi.dtype),
        in_specs=[smem] * 4 + [hbm] * 2,
        out_specs=hbm,
        scratch_shapes=[pltpu.SMEM((PLACES,), jnp.int32), pltpu.SemaphoreType.DMA],
    )(where, term_order, connect, sector_at, own, other)
    blocks = lax.all_to_all(chosen, "term", 0, 0, tiled=True).reshape(GROUPS, SLOTS, PART, BLK)
    summed = pl.pallas_call(
        product_kernel,
        grid=(SLOTS,),
        out_shape=jax.ShapeDtypeStruct((BLK, BLK), jnp.float32),
        in_specs=[smem] * 5
        + [
            pl.BlockSpec((GROUPS, 1, PART, BLK), lambda k: (0, k, 0, 0)),
            pl.BlockSpec((1, 1, BLK, BLK), lambda k: (k, 0, 0, 0)),
            pl.BlockSpec((1, BLK, BLK), lambda k: (k, 0, 0)),
        ],
        out_specs=pl.BlockSpec((BLK, BLK), lambda k: (0, 0)),
        scratch_shapes=[pltpu.VMEM((BLK, BLK), jnp.float32)],
        compiler_params=pltpu.CompilerParams(vmem_limit_bytes=32 * 1024 * 1024),
    )(where, term_order, connect, sector_at, sector_rows, blocks, left_blocks, right_ops)
    parts = lax.all_to_all(summed.reshape(GROUPS, PART, BLK), "term", 0, 0, tiled=True)
    return jnp.sum(parts, axis=0).T[None]


def solution(mesh):
    placed = (
        P("sector", None, None),
        P("term", "sector", None, None),
        P("term", None, None),
        P(),
        P(),
        P(),
        P(),
    )
    return jax.shard_map(
        on_device, mesh=mesh, in_specs=placed, out_specs=P("sector", None, "term"), check_vma=False
    )
```

```python
import functools

import jax
import jax.numpy as jnp
from jax import lax
from jax.experimental import pallas as pl
from jax.experimental.pallas import tpu as pltpu
from jax.sharding import PartitionSpec as P

GROUPS = 8
SLOTS = 8
PLACES = 32
BLK = 512
PART = BLK // GROUPS


def place_permutation(f):
    return [(s, f(s)) for s in range(PLACES)]


def find_positions(sector_at, position):
    def put(p, carry):
        position[sector_at[p]] = p
        return carry

    lax.fori_loop(0, PLACES, put, 0)


def select_kernel(where, term_order, connect, sector_at, own, other, out, position):
    find_positions(sector_at, position)
    place = where[1]
    core = lax.rem(place, 2)
    target = sector_at[place]

    def start(i, carry):
        p = position[connect[term_order[i], target]]
        half = lax.div(p, 2)
        mine = lax.rem(p, 2) == core

        @pl.when(mine)
        def _():
            out[i] = own[half]

        @pl.when(jnp.logical_not(mine))
        def _():
            out[i] = other[half]

        return carry

    lax.fori_loop(0, GROUPS * SLOTS, start, 0)


def product_kernel(where, term_order, connect, sector_at, sector_rows, block, left, right, out, acc):
    k = pl.program_id(0)
    group, place = where[0], where[1]
    target = sector_at[place]
    source = connect[term_order[group * SLOTS + k], target]
    live = sector_rows[source]
    rows = lax.broadcasted_iota(jnp.int32, (BLK, BLK), 0)
    b = block[...].reshape(BLK, BLK)
    b = jnp.where(rows < live, b, jnp.zeros((), b.dtype))
    t = jnp.dot(b, right[0], preferred_element_type=jnp.float32)
    hi = t.astype(jnp.bfloat16)
    lo = (t - hi.astype(jnp.float32)).astype(jnp.bfloat16)
    l = left[0, 0]
    part = jnp.dot(l, hi, preferred_element_type=jnp.float32) + jnp.dot(
        l, lo, preferred_element_type=jnp.float32
    )

    @pl.when(k == 0)
    def _():
        acc[...] = part

    @pl.when(k > 0)
    def _():
        acc[...] += part

    @pl.when(k == SLOTS - 1)
    def _():
        total = jnp.where(rows < sector_rows[target], acc[...], 0.0)
        out[...] = total.T


def on_device(psi, left_blocks, right_ops, sector_rows, connect, term_order, sector_at):
    group = lax.axis_index("term")
    place = lax.axis_index("sector")
    where = jnp.stack([group, place]).astype(jnp.int32)
    smem = pl.BlockSpec(memory_space=pltpu.SMEM)
    vmem = pl.BlockSpec(memory_space=pltpu.VMEM)

    part = lax.dynamic_slice_in_dim(psi[0], group * PART, PART)
    copies = jnp.broadcast_to(part[None], (PLACES // 2, PART, BLK))
    same_core = [[c + 2 * h for h in range(PLACES // 2)] for c in range(2)]
    own = lax.all_to_all(copies, "sector", 0, 0, axis_index_groups=same_core, tiled=True)
    other = lax.ppermute(own, "sector", place_permutation(lambda s: s ^ 1))
    chosen = pl.pallas_call(
        select_kernel,
        out_shape=jax.ShapeDtypeStruct((GROUPS * SLOTS, PART, BLK), psi.dtype),
        in_specs=[smem] * 4 + [vmem] * 2,
        out_specs=vmem,
        scratch_shapes=[pltpu.SMEM((PLACES,), jnp.int32)],
        compiler_params=pltpu.CompilerParams(vmem_limit_bytes=32 * 1024 * 1024),
    )(where, term_order, connect, sector_at, own, other)
    blocks = lax.all_to_all(chosen, "term", 0, 0, tiled=True).reshape(GROUPS, SLOTS, PART, BLK)
    summed = pl.pallas_call(
        product_kernel,
        grid=(SLOTS,),
        out_shape=jax.ShapeDtypeStruct((BLK, BLK), jnp.float32),
        in_specs=[smem] * 5
        + [
            pl.BlockSpec((GROUPS, 1, PART, BLK), lambda k: (0, k, 0, 0)),
            pl.BlockSpec((1, 1, BLK, BLK), lambda k: (k, 0, 0, 0)),
            pl.BlockSpec((1, BLK, BLK), lambda k: (k, 0, 0)),
        ],
        out_specs=pl.BlockSpec((BLK, BLK), lambda k: (0, 0)),
        scratch_shapes=[pltpu.VMEM((BLK, BLK), jnp.float32)],
        compiler_params=pltpu.CompilerParams(vmem_limit_bytes=32 * 1024 * 1024),
    )(where, term_order, connect, sector_at, sector_rows, blocks, left_blocks, right_ops)
    parts = lax.all_to_all(summed.reshape(GROUPS, PART, BLK), "term", 0, 0, tiled=True)
    return jnp.sum(parts, axis=0).T[None]


def solution(mesh):
    placed = (
        P("sector", None, None),
        P("term", "sector", None, None),
        P("term", None, None),
        P(),
        P(),
        P(),
        P(),
    )
    return jax.shard_map(
        on_device, mesh=mesh, in_specs=placed, out_specs=P("sector", None, "term"), check_vma=False
    )
```

```python
import functools

import jax
import jax.numpy as jnp
from jax import lax
from jax.experimental import pallas as pl
from jax.experimental.pallas import tpu as pltpu
from jax.sharding import PartitionSpec as P

GROUPS = 8
SLOTS = 8
PLACES = 32
BLK = 512
PEERS = 16
FRONT = 256
REST = BLK - FRONT
TALL = FRONT // 4
WIDE = BLK // 4
BOTH = ("term", "sector")
VMEM_LIMIT = 48 * 1024 * 1024


def flat(t, s):
    return t * PLACES + s


def place_of(h, z, c):
    return (h * 8 + z % 8) * 2 + c


def pairs(f):
    return [(flat(t, s), f(t, s)) for t in range(GROUPS) for s in range(PLACES)]


def ring_target(t, s):
    h, z, c = s // 16, s // 2 % 8, s % 2
    return flat(t, place_of(h, z + 1 - 2 * c, c))


FAR = pairs(lambda t, s: flat(t ^ 1, s ^ 16))
SWAP = pairs(lambda t, s: flat(t, s ^ 1))
RING = pairs(ring_target)
SAME_CORE = [[place_of(h, z, c) for h in range(2) for z in range(8)] for c in range(2)]
PEER_GROUPS = [
    [flat(t, place_of(h, z, c)) for t in range(GROUPS) for h in range(2)]
    for z in range(8)
    for c in range(2)
]


def index_kernel(term_order, connect, sector_at, sector_rows, front, mine, position):
    group, place = lax.axis_index("term"), lax.axis_index("sector")
    core = lax.rem(place, 2)
    half = lax.div(place, 16)
    z = lax.rem(lax.div(place, 2), 8)

    def put(p, carry):
        position[sector_at[p]] = p
        return carry

    lax.fori_loop(0, PLACES, put, 0)

    def note(k, carry):
        source = connect[sector_at[place], term_order[group * SLOTS + k]]
        p = position[source]
        step = lax.rem(lax.div(p, 2), 8) - z
        step = lax.rem(jnp.where(core == 0, -step, step) + 8, 8)
        mine[0, k] = step * 2 + jnp.where(lax.rem(p, 2) == core, 0, 1)
        mine[1, k] = jnp.where(lax.div(p, 16) == half, 0, 1)
        mine[2, k] = sector_rows[source]
        mine[3, k] = sector_rows[sector_at[place]]
        return carry

    lax.fori_loop(0, SLOTS, note, 0)

    def peer(m, carry):
        their_group = lax.div(m, 2)
        target = sector_at[lax.rem(m, 2) * 16 + lax.rem(place, 16)]

        def slot(k, carry):
            p = position[connect[target, term_order[their_group * SLOTS + k]]]
            front[m * SLOTS + k] = lax.div(p, 2) + jnp.where(lax.rem(p, 2) == core, 0, 16)
            return carry

        return lax.fori_loop(0, SLOTS, slot, carry)

    lax.fori_loop(0, PEERS, peer, 0)


def select_kernel(front, own, other, out):
    def slot(i, carry):
        at = front[i]

        @pl.when(at < 16)
        def _():
            out[i] = own[at]

        @pl.when(at >= 16)
        def _():
            out[i] = other[at - 16]

        return carry

    lax.fori_loop(0, PEERS * SLOTS, slot, 0, unroll=8)


def product_kernel(mine, front, left, right, *refs):
    blocks, (out, held, block, acc, sem) = refs[:PEERS], refs[PEERS:]
    k = pl.program_id(0)

    def fetch(j):
        for i, ref in enumerate(blocks):

            @pl.when(mine[0, j] == i)
            def _(ref=ref):
                slot = lax.rem(j, 2)
                pltpu.make_async_copy(ref.at[mine[1, j]], held.at[slot], sem.at[slot]).start()

    @pl.when(k == 0)
    def _():
        fetch(0)

    @pl.when(k < SLOTS - 1)
    def _():
        fetch(k + 1)

    now = lax.rem(k, 2)
    pltpu.make_async_copy(held.at[now], held.at[now], sem.at[now]).wait()
    live = mine[2, k]

    def rows(first, count):
        return lax.broadcasted_iota(jnp.int32, (count, BLK), 0) + first

    for m in range(PEERS):
        block[m // 4 * TALL : (m // 4 + 1) * TALL, m % 4 * WIDE : (m % 4 + 1) * WIDE] = front[m, 0]
    block[FRONT:, :] = held[now]
    b = block[...]
    b = jnp.where(rows(0, BLK) < live, b, jnp.zeros((), b.dtype))
    t = jnp.dot(b, right[0], preferred_element_type=jnp.float32)
    hi = t.astype(jnp.bfloat16)
    lo = (t - hi.astype(jnp.float32)).astype(jnp.bfloat16)
    part = jnp.dot(left[0, 0], hi, preferred_element_type=jnp.float32)
    part = part + jnp.dot(left[0, 0], lo, preferred_element_type=jnp.float32)

    @pl.when(k == 0)
    def _():
        acc[...] = part

    @pl.when(k > 0)
    def _():
        acc[...] += part

    @pl.when(k == SLOTS - 1)
    def _():
        out[...] = jnp.where(rows(0, BLK) < mine[3, 0], acc[...], 0.0).T


def on_device(psi, left_blocks, right_ops, sector_rows, connect, term_order, sector_at):
    group = lax.axis_index("term")
    smem = pl.BlockSpec(memory_space=pltpu.SMEM)
    vmem = pl.BlockSpec(memory_space=pltpu.VMEM)
    params = pltpu.CompilerParams(vmem_limit_bytes=VMEM_LIMIT)
    psi = psi[0]

    def hop(x, perm):
        return lax.ppermute(x, BOTH, perm)

    front_index, mine = pl.pallas_call(
        index_kernel,
        out_shape=(
            jax.ShapeDtypeStruct((PEERS * SLOTS,), jnp.int32),
            jax.ShapeDtypeStruct((4, SLOTS), jnp.int32),
        ),
        in_specs=[smem] * 4,
        out_specs=(smem, smem),
        scratch_shapes=[pltpu.SMEM((PLACES,), jnp.int32)],
        cost_estimate=pl.CostEstimate(flops=0, bytes_accessed=8 * 1024 * 1024, transcendentals=0),
    )(term_order, connect.T, sector_at, sector_rows)

    def chunk(h):
        m = group * 2 + h
        return lax.dynamic_slice(psi, (m // 4 * TALL, m % 4 * WIDE), (TALL, WIDE))

    copies = jnp.broadcast_to(jnp.stack([chunk(0), chunk(1)])[:, None], (2, 8, TALL, WIDE))
    own = lax.all_to_all(
        copies.reshape(PEERS, TALL, WIDE), "sector", 0, 0, axis_index_groups=SAME_CORE, tiled=True
    )
    own, front_index = lax.optimization_barrier((own, front_index))
    other = hop(own, SWAP)
    chosen = pl.pallas_call(
        select_kernel,
        out_shape=jax.ShapeDtypeStruct((PEERS * SLOTS, TALL, WIDE), psi.dtype),
        in_specs=[smem] + [vmem] * 2,
        out_specs=vmem,
        compiler_params=params,
    )(front_index, own, other)
    front = lax.all_to_all(chosen, BOTH, 0, 0, axis_index_groups=PEER_GROUPS, tiled=True)
    front = front.reshape(PEERS, SLOTS, TALL, WIDE)

    x = [jnp.stack([psi[FRONT:], hop(psi[FRONT:], FAR)])]
    y = [hop(x[0], SWAP)]
    for step in range(1, 5):
        x.append(hop(x[-1], RING))
        if step < 4:
            y.append(hop(y[-1], RING))
    x_swapped = [None] + [hop(v, SWAP) for v in x[1:]]
    y_swapped = [None] + [hop(v, SWAP) for v in y[1:]]
    blocks = []
    for step in range(4):
        blocks += [x[step], y[step]]
    blocks += [x[4], x_swapped[4]]
    for step in (3, 2, 1):
        blocks += [y_swapped[step], x_swapped[step]]

    summed = pl.pallas_call(
        product_kernel,
        out_shape=jax.ShapeDtypeStruct((BLK, BLK), jnp.float32),
        grid_spec=pltpu.PrefetchScalarGridSpec(
            num_scalar_prefetch=1,
            grid=(SLOTS,),
            in_specs=[
                pl.BlockSpec((PEERS, 1, TALL, WIDE), lambda k, mine: (0, k, 0, 0)),
                pl.BlockSpec((1, 1, BLK, BLK), lambda k, mine: (k, 0, 0, 0)),
                pl.BlockSpec((1, BLK, BLK), lambda k, mine: (k, 0, 0)),
            ]
            + [pl.BlockSpec(memory_space=pl.ANY)] * PEERS,
            out_specs=pl.BlockSpec((BLK, BLK), lambda k, mine: (0, 0)),
            scratch_shapes=[
                pltpu.VMEM((2, REST, BLK), jnp.bfloat16),
                pltpu.VMEM((BLK, BLK), jnp.bfloat16),
                pltpu.VMEM((BLK, BLK), jnp.float32),
                pltpu.SemaphoreType.DMA((2,)),
            ],
        ),
        compiler_params=params,
    )(mine, front, left_blocks, right_ops, *blocks)
    parts = lax.all_to_all(
        summed.reshape(GROUPS, BLK // GROUPS, BLK), "term", 0, 0, tiled=True
    )
    return jnp.sum(parts, axis=0).T[None]


def solution(mesh):
    placed = (
        P("sector", None, None),
        P("term", "sector", None, None),
        P("term", None, None),
        P(),
        P(),
        P(),
        P(),
    )
    return jax.shard_map(
        on_device, mesh=mesh, in_specs=placed, out_specs=P("sector", None, "term"), check_vma=False
    )
```

```python
import functools

import jax
import jax.numpy as jnp
from jax import lax
from jax.experimental import pallas as pl
from jax.experimental.pallas import tpu as pltpu
from jax.sharding import PartitionSpec as P

GROUPS = 8
SLOTS = 8
PLACES = 32
BLK = 512
PEERS = 16
FRONT = 256
REST = BLK - FRONT
PART = FRONT // PEERS
BOTH = ("term", "sector")
LN2 = 0.6931471805599453
LEVELS = 64.0
STEPS = 32766.0
VMEM_LIMIT = 48 * 1024 * 1024


def flat(t, s):
    return t * PLACES + s


def place_of(h, z, c):
    return (h * 8 + z % 8) * 2 + c


def pairs(f):
    return [(flat(t, s), f(t, s)) for t in range(GROUPS) for s in range(PLACES)]


def ring_target(t, s):
    h, z, c = s // 16, s // 2 % 8, s % 2
    return flat(t, place_of(h, z + 1 - 2 * c, c))


FAR = pairs(lambda t, s: flat(t ^ 1, s ^ 16))
SWAP = pairs(lambda t, s: flat(t, s ^ 1))
RING = pairs(ring_target)
SAME_CORE = [[place_of(h, z, c) for h in range(2) for z in range(8)] for c in range(2)]
PEER_GROUPS = [
    [flat(t, place_of(h, z, c)) for t in range(GROUPS) for h in range(2)]
    for z in range(8)
    for c in range(2)
]


def index_kernel(term_order, connect, sector_at, sector_rows, front, mine, position):
    group, place = lax.axis_index("term"), lax.axis_index("sector")
    core = lax.rem(place, 2)
    half = lax.div(place, 16)
    z = lax.rem(lax.div(place, 2), 8)

    def put(p, carry):
        position[sector_at[p]] = p
        return carry

    lax.fori_loop(0, PLACES, put, 0)

    def note(k, carry):
        source = connect[sector_at[place], term_order[group * SLOTS + k]]
        p = position[source]
        step = lax.rem(lax.div(p, 2), 8) - z
        step = lax.rem(jnp.where(core == 0, -step, step) + 8, 8)
        side = jnp.where(lax.div(p, 16) == half, 0, 1)
        parity = jnp.where(lax.rem(p, 2) == core, 0, 1)
        mine[0, k] = step * 2 + parity
        mine[1, k] = side
        mine[2, k] = sector_rows[source]
        mine[3, k] = sector_rows[sector_at[place]]
        return carry

    lax.fori_loop(0, SLOTS, note, 0)

    def peer(m, carry):
        their_group = lax.div(m, 2)
        target = sector_at[lax.rem(m, 2) * 16 + lax.rem(place, 16)]

        def slot(k, carry):
            p = position[connect[target, term_order[their_group * SLOTS + k]]]
            front[m * SLOTS + k] = lax.div(p, 2) + jnp.where(lax.rem(p, 2) == core, 0, 16)
            return carry

        return lax.fori_loop(0, SLOTS, slot, carry)

    lax.fori_loop(0, PEERS, peer, 0)


def select_kernel(front, own, other, out, held, sem):
    def peer(m, carry):
        for k in range(SLOTS):
            at = front[m * SLOTS + k]

            @pl.when(at < 16)
            def _(k=k, at=at):
                held[m, k] = own[at]

            @pl.when(at >= 16)
            def _(k=k, at=at):
                held[m, k] = other[at - 16]

        pltpu.make_async_copy(held.at[m], out.at[m], sem).start()
        return carry

    lax.fori_loop(0, PEERS, peer, 0)
    pltpu.make_async_copy(held, out, sem).wait()


def product_kernel(mine, front, left, right, *refs):
    blocks, refs = refs[:PEERS], refs[PEERS:]
    out, fronts, rests, lefts, rights, block, acc, front_sem, rest_sem, left_sem, right_sem = refs

    def fetch(j, carry):
        pltpu.make_async_copy(right.at[j], rights.at[j], right_sem.at[j]).start()
        pltpu.make_async_copy(front.at[:, j], fronts.at[j], front_sem.at[j]).start()
        for i, ref in enumerate(blocks):

            @pl.when(mine[0, j] == i)
            def _(ref=ref):
                pltpu.make_async_copy(ref.at[mine[1, j]], rests.at[j], rest_sem.at[j]).start()

        pltpu.make_async_copy(left.at[j, 0], lefts.at[j], left_sem.at[j]).start()
        return carry

    lax.fori_loop(0, SLOTS, fetch, 0)

    def arrived(buffer, sem, k):
        pltpu.make_async_copy(buffer.at[k], buffer.at[k], sem.at[k]).wait()
        return buffer[k]

    def dot(a, b):
        return jnp.dot(a, b, preferred_element_type=jnp.float32)

    rows = lax.broadcasted_iota(jnp.int32, (BLK, BLK), 0)
    for k in range(SLOTS):
        block[k % 2, :FRONT] = arrived(fronts, front_sem, k).reshape(FRONT, BLK)
        block[k % 2, FRONT:] = arrived(rests, rest_sem, k)
        t = dot(block[k % 2], arrived(rights, right_sem, k))
        t = jnp.where(rows < mine[2, k], t, 0.0)
        hi = t.astype(jnp.bfloat16)
        lo = (t - hi.astype(jnp.float32)).astype(jnp.bfloat16)
        left_k = arrived(lefts, left_sem, k)
        part = dot(left_k, hi) + dot(left_k, lo)
        if k == 0:
            acc[...] = part
        else:
            acc[...] += part
    total = jnp.where(rows < mine[3, 0], acc[...], 0.0).T
    largest = jnp.maximum(jnp.max(jnp.abs(total), axis=1, keepdims=True), 1e-30)
    level = jnp.ceil(jnp.log(largest) * (LEVELS / LN2)) + 1.0
    steps = total * (STEPS * jnp.exp(level * (-LN2 / LEVELS)))
    out[:, :BLK] = jnp.round(steps).astype(jnp.int32).astype(jnp.int16)
    out[:, BLK:] = jnp.broadcast_to(level, (BLK, 128)).astype(jnp.int32).astype(jnp.int16)


def total_kernel(parts, out):
    total = None
    for g in range(GROUPS):
        level = parts[g, :, BLK:].astype(jnp.int32).astype(jnp.float32)[:, :1]
        size = jnp.exp(level * (LN2 / LEVELS)) * (1.0 / STEPS)
        part = parts[g, :, :BLK].astype(jnp.int32).astype(jnp.float32) * size
        total = part if total is None else total + part
    out[...] = total


def on_device(psi, left_blocks, right_ops, sector_rows, connect, term_order, sector_at):
    group = lax.axis_index("term")
    smem = pl.BlockSpec(memory_space=pltpu.SMEM)
    vmem = pl.BlockSpec(memory_space=pltpu.VMEM)
    anywhere = pl.BlockSpec(memory_space=pl.ANY)
    params = pltpu.CompilerParams(vmem_limit_bytes=VMEM_LIMIT)
    psi = psi[0]

    def hop(x, perm):
        return lax.ppermute(x, BOTH, perm)

    front_index, mine = pl.pallas_call(
        index_kernel,
        out_shape=(
            jax.ShapeDtypeStruct((PEERS * SLOTS,), jnp.int32),
            jax.ShapeDtypeStruct((4, SLOTS), jnp.int32),
        ),
        in_specs=[smem] * 4,
        out_specs=(smem, smem),
        scratch_shapes=[pltpu.SMEM((PLACES,), jnp.int32)],
        cost_estimate=pl.CostEstimate(flops=0, bytes_accessed=8 * 1024 * 1024, transcendentals=0),
    )(term_order, connect.T, sector_at, sector_rows)

    def after(x, y):
        return lax.optimization_barrier((x, y))[0]

    x = [jnp.stack([psi[FRONT:], hop(psi[FRONT:], FAR)])]
    y = [hop(x[0], SWAP)]
    pieces = lax.dynamic_slice(psi, (group * 2 * PART, 0), (2 * PART, BLK)).reshape(2, 1, PART, BLK)
    copies = jnp.broadcast_to(pieces, (2, PLACES // 4, PART, BLK)).reshape(PEERS, PART, BLK)
    own = lax.all_to_all(copies, "sector", 0, 0, axis_index_groups=SAME_CORE, tiled=True)
    own = after(own, front_index)
    other = hop(own, SWAP)
    chosen = pl.pallas_call(
        select_kernel,
        out_shape=pltpu.HBM((PEERS, SLOTS, PART, BLK), psi.dtype),
        in_specs=[smem] + [vmem] * 2,
        out_specs=anywhere,
        scratch_shapes=[
            pltpu.VMEM((PEERS, SLOTS, PART, BLK), psi.dtype),
            pltpu.SemaphoreType.DMA,
        ],
        cost_estimate=pl.CostEstimate(flops=0, bytes_accessed=8 * 1024 * 1024, transcendentals=0),
        compiler_params=params,
    )(front_index, own, other)
    front = lax.all_to_all(chosen, BOTH, 0, 0, axis_index_groups=PEER_GROUPS, tiled=True)
    for step in range(1, 5):
        x.append(hop(x[-1], RING))
        if step < 4:
            y.append(hop(y[-1], RING))
    x_swapped = [None] + [hop(v, SWAP) for v in x[1:]]
    y_swapped = [None] + [hop(v, SWAP) for v in y[1:]]
    blocks = []
    for step in range(4):
        blocks += [x[step], y[step]]
    blocks += [x[4], x_swapped[4]]
    for step in (3, 2, 1):
        blocks += [y_swapped[step], x_swapped[step]]

    summed = pl.pallas_call(
        product_kernel,
        out_shape=jax.ShapeDtypeStruct((BLK, BLK + 128), jnp.int16),
        in_specs=[smem] + [anywhere] * (3 + PEERS),
        out_specs=vmem,
        scratch_shapes=[
            pltpu.VMEM((SLOTS, PEERS, PART, BLK), jnp.bfloat16),
            pltpu.VMEM((SLOTS, REST, BLK), jnp.bfloat16),
            pltpu.VMEM((SLOTS, BLK, BLK), jnp.bfloat16),
            pltpu.VMEM((SLOTS, BLK, BLK), jnp.bfloat16),
            pltpu.VMEM((2, BLK, BLK), jnp.bfloat16),
            pltpu.VMEM((BLK, BLK), jnp.float32),
        ]
        + [pltpu.SemaphoreType.DMA((SLOTS,))] * 4,
        compiler_params=params,
    )(
        mine,
        front,
        left_blocks,
        right_ops,
        *[pltpu.with_memory_space_constraint(b, pltpu.HBM) for b in blocks],
    )
    parts = lax.all_to_all(
        summed.reshape(GROUPS, BLK // GROUPS, BLK + 128), "term", 0, 0, tiled=True
    )
    total = pl.pallas_call(
        total_kernel,
        out_shape=jax.ShapeDtypeStruct((BLK // GROUPS, BLK), jnp.float32),
        in_specs=[vmem],
        out_specs=vmem,
    )(parts)
    return total.T[None]


def solution(mesh):
    placed = (
        P("sector", None, None),
        P("term", "sector", None, None),
        P("term", None, None),
        P(),
        P(),
        P(),
        P(),
    )
    return jax.shard_map(
        on_device, mesh=mesh, in_specs=placed, out_specs=P("sector", None, "term"), check_vma=False
    )
```

```python
import functools

import jax
import jax.numpy as jnp
from jax import lax
from jax.experimental import pallas as pl
from jax.experimental.pallas import tpu as pltpu
from jax.sharding import PartitionSpec as P

GROUPS = 8
SLOTS = 8
PLACES = 32
BLK = 512
PEERS = 16
FRONT = 256
REST = BLK - FRONT
PART = FRONT // PEERS
BOTH = ("term", "sector")
LN2 = 0.6931471805599453
LEVELS = 64.0
STEPS = 32766.0
WIDTH = BLK // GROUPS
VMEM_LIMIT = 48 * 1024 * 1024


def flat(t, s):
    return t * PLACES + s


def place_of(h, z, c):
    return (h * 8 + z % 8) * 2 + c


def pairs(f):
    return [(flat(t, s), f(t, s)) for t in range(GROUPS) for s in range(PLACES)]


def ring_target(t, s):
    h, z, c = s // 16, s // 2 % 8, s % 2
    return flat(t, place_of(h, z + 1 - 2 * c, c))


FAR = pairs(lambda t, s: flat(t ^ 1, s ^ 16))
SWAP = pairs(lambda t, s: flat(t, s ^ 1))
RING = pairs(ring_target)
SAME_CORE = [[place_of(h, z, c) for h in range(2) for z in range(8)] for c in range(2)]
PEER_GROUPS = [
    [flat(t, place_of(h, z, c)) for t in range(GROUPS) for h in range(2)]
    for z in range(8)
    for c in range(2)
]


def index_kernel(term_order, connect, sector_at, sector_rows, front, mine, position):
    group, place = lax.axis_index("term"), lax.axis_index("sector")
    core = lax.rem(place, 2)
    half = lax.div(place, 16)
    z = lax.rem(lax.div(place, 2), 8)

    def put(p, carry):
        position[sector_at[p]] = p
        return carry

    lax.fori_loop(0, PLACES, put, 0)

    def note(k, carry):
        source = connect[sector_at[place], term_order[group * SLOTS + k]]
        p = position[source]
        step = lax.rem(lax.div(p, 2), 8) - z
        step = lax.rem(jnp.where(core == 0, -step, step) + 8, 8)
        side = jnp.where(lax.div(p, 16) == half, 0, 1)
        parity = jnp.where(lax.rem(p, 2) == core, 0, 1)
        mine[0, k] = step * 2 + parity
        mine[1, k] = side
        mine[2, k] = sector_rows[source]
        mine[3, k] = sector_rows[sector_at[place]]
        return carry

    lax.fori_loop(0, SLOTS, note, 0)

    def peer(m, carry):
        their_group = lax.div(m, 2)
        target = sector_at[lax.rem(m, 2) * 16 + lax.rem(place, 16)]

        def slot(k, carry):
            p = position[connect[target, term_order[their_group * SLOTS + k]]]
            front[m * SLOTS + k] = lax.div(p, 2) + jnp.where(lax.rem(p, 2) == core, 0, 16)
            return carry

        return lax.fori_loop(0, SLOTS, slot, carry)

    lax.fori_loop(0, PEERS, peer, 0)


def select_kernel(front, own, other, out, both, held, sem):
    both[:16] = own[...]
    both[16:] = other[...]

    def peer(m, carry):
        for k in range(SLOTS):
            held[m, k] = both[front[m * SLOTS + k]]
        pltpu.make_async_copy(held.at[m], out.at[m], sem).start()
        return carry

    lax.fori_loop(0, PEERS, peer, 0)
    pltpu.make_async_copy(held, out, sem).wait()


def product_kernel(mine, front, left, right, *refs):
    blocks, refs = refs[:PEERS], refs[PEERS:]
    out, fronts, rests, lefts, rights, block, acc, front_sem, rest_sem, left_sem, right_sem = refs

    def fetch_rest(j, low, high):
        if high - low == 1:
            ref = blocks[low]
            pltpu.make_async_copy(ref.at[mine[1, j]], rests.at[j], rest_sem.at[j]).start()
            return
        middle = (low + high) // 2
        below = mine[0, j] < middle

        @pl.when(below)
        def _():
            fetch_rest(j, low, middle)

        @pl.when(jnp.logical_not(below))
        def _():
            fetch_rest(j, middle, high)

    def fetch(j, carry):
        pltpu.make_async_copy(right.at[j], rights.at[j], right_sem.at[j]).start()
        pltpu.make_async_copy(front.at[:, j], fronts.at[j], front_sem.at[j]).start()
        fetch_rest(j, 0, PEERS)
        pltpu.make_async_copy(left.at[j, 0], lefts.at[j], left_sem.at[j]).start()
        return carry

    lax.fori_loop(0, SLOTS, fetch, 0)

    def arrived(buffer, sem, k):
        pltpu.make_async_copy(buffer.at[k], buffer.at[k], sem.at[k]).wait()
        return buffer[k]

    def dot(a, b):
        return jnp.dot(a, b, preferred_element_type=jnp.float32)

    rows = lax.broadcasted_iota(jnp.int32, (BLK, BLK), 0)
    for k in range(SLOTS):
        block[k % 2, :FRONT] = arrived(fronts, front_sem, k).reshape(FRONT, BLK)
        block[k % 2, FRONT:] = arrived(rests, rest_sem, k)
        t = dot(block[k % 2], arrived(rights, right_sem, k))
        t = jnp.where(rows < mine[2, k], t, 0.0)
        hi = t.astype(jnp.bfloat16)
        lo = (t - hi.astype(jnp.float32)).astype(jnp.bfloat16)
        left_k = arrived(lefts, left_sem, k)
        part = dot(left_k, hi) + dot(left_k, lo)
        if k == 0:
            acc[...] = part
        else:
            acc[...] += part
    total = jnp.where(rows < mine[3, 0], acc[...], 0.0).T
    for g in range(GROUPS):
        piece = total[g * WIDTH : (g + 1) * WIDTH]
        largest = jnp.maximum(jnp.max(jnp.abs(piece), axis=0, keepdims=True), 1e-30)
        level = jnp.ceil(jnp.log(largest) * (LEVELS / LN2)) + 1.0
        steps = piece * (STEPS * jnp.exp(level * (-LN2 / LEVELS)))
        out[g, :WIDTH] = jnp.round(steps).astype(jnp.int32).astype(jnp.int16)
        out[g, WIDTH:] = jnp.broadcast_to(level, (16, BLK)).astype(jnp.int32).astype(jnp.int16)


def on_device(psi, left_blocks, right_ops, sector_rows, connect, term_order, sector_at):
    group = lax.axis_index("term")
    smem = pl.BlockSpec(memory_space=pltpu.SMEM)
    vmem = pl.BlockSpec(memory_space=pltpu.VMEM)
    anywhere = pl.BlockSpec(memory_space=pl.ANY)
    params = pltpu.CompilerParams(vmem_limit_bytes=VMEM_LIMIT)
    psi = psi[0]

    def hop(x, perm):
        return lax.ppermute(x, BOTH, perm)

    front_index, mine = pl.pallas_call(
        index_kernel,
        out_shape=(
            jax.ShapeDtypeStruct((PEERS * SLOTS,), jnp.int32),
            jax.ShapeDtypeStruct((4, SLOTS), jnp.int32),
        ),
        in_specs=[smem] * 4,
        out_specs=(smem, smem),
        scratch_shapes=[pltpu.SMEM((PLACES,), jnp.int32)],
        cost_estimate=pl.CostEstimate(flops=0, bytes_accessed=8 * 1024 * 1024, transcendentals=0),
    )(term_order, connect.T, sector_at, sector_rows)

    def after(x, y):
        return lax.optimization_barrier((x, y))[0]

    x = [jnp.stack([psi[FRONT:], hop(psi[FRONT:], FAR)])]
    y = [hop(x[0], SWAP)]
    pieces = lax.dynamic_slice(psi, (group * 2 * PART, 0), (2 * PART, BLK)).reshape(2, 1, PART, BLK)
    copies = jnp.broadcast_to(pieces, (2, PLACES // 4, PART, BLK)).reshape(PEERS, PART, BLK)
    own = lax.all_to_all(copies, "sector", 0, 0, axis_index_groups=SAME_CORE, tiled=True)
    own = after(own, front_index)
    other = hop(own, SWAP)
    chosen = pl.pallas_call(
        select_kernel,
        out_shape=pltpu.HBM((PEERS, SLOTS, PART, BLK), psi.dtype),
        in_specs=[smem] + [vmem] * 2,
        out_specs=anywhere,
        scratch_shapes=[
            pltpu.VMEM((PLACES, PART, BLK), psi.dtype),
            pltpu.VMEM((PEERS, SLOTS, PART, BLK), psi.dtype),
            pltpu.SemaphoreType.DMA,
        ],
        cost_estimate=pl.CostEstimate(flops=0, bytes_accessed=8 * 1024 * 1024, transcendentals=0),
        compiler_params=params,
    )(front_index, own, other)
    front = lax.all_to_all(chosen, BOTH, 0, 0, axis_index_groups=PEER_GROUPS, tiled=True)
    for step in range(1, 5):
        x.append(hop(x[-1], RING))
        if step < 4:
            y.append(hop(y[-1], RING))
    x_swapped = [None] + [hop(v, SWAP) for v in x[1:]]
    y_swapped = [None] + [hop(v, SWAP) for v in y[1:]]
    blocks = []
    for step in range(4):
        blocks += [x[step], y[step]]
    blocks += [x[4], x_swapped[4]]
    for step in (3, 2, 1):
        blocks += [y_swapped[step], x_swapped[step]]

    summed = pl.pallas_call(
        product_kernel,
        out_shape=jax.ShapeDtypeStruct((GROUPS, WIDTH + 16, BLK), jnp.int16),
        in_specs=[smem] + [anywhere] * (3 + PEERS),
        out_specs=vmem,
        scratch_shapes=[
            pltpu.VMEM((SLOTS, PEERS, PART, BLK), jnp.bfloat16),
            pltpu.VMEM((SLOTS, REST, BLK), jnp.bfloat16),
            pltpu.VMEM((SLOTS, BLK, BLK), jnp.bfloat16),
            pltpu.VMEM((SLOTS, BLK, BLK), jnp.bfloat16),
            pltpu.VMEM((2, BLK, BLK), jnp.bfloat16),
            pltpu.VMEM((BLK, BLK), jnp.float32),
        ]
        + [pltpu.SemaphoreType.DMA((SLOTS,))] * 4,
        compiler_params=params,
    )(
        mine,
        front,
        left_blocks,
        right_ops,
        *[pltpu.with_memory_space_constraint(b, pltpu.HBM) for b in blocks],
    )
    parts = lax.all_to_all(summed, "term", 0, 0, tiled=True).astype(jnp.float32)
    sizes = jnp.exp(parts[:, WIDTH:WIDTH + 1] * (LN2 / LEVELS)) * (1.0 / STEPS)
    return jnp.sum(parts[:, :WIDTH] * sizes, axis=0).T[None]


def solution(mesh):
    placed = (
        P("sector", None, None),
        P("term", "sector", None, None),
        P("term", None, None),
        P(),
        P(),
        P(),
        P(),
    )
    return jax.shard_map(
        on_device, mesh=mesh, in_specs=placed, out_specs=P("sector", None, "term"), check_vma=False
    )
```

```python
import functools

import jax
import jax.numpy as jnp
from jax import lax
from jax.experimental import pallas as pl
from jax.experimental.pallas import tpu as pltpu
from jax.sharding import PartitionSpec as P

GROUPS = 8
SLOTS = 8
PLACES = 32
BLK = 512
PEERS = 16
FRONT = 256
REST = BLK - FRONT
PART = FRONT // PEERS
BOTH = ("term", "sector")
LN2 = 0.6931471805599453
LEVELS = 64.0
STEPS = 32766.0
WIDTH = BLK // GROUPS
VMEM_LIMIT = 48 * 1024 * 1024


def flat(t, s):
    return t * PLACES + s


def place_of(h, z, c):
    return (h * 8 + z % 8) * 2 + c


def pairs(f):
    return [(flat(t, s), f(t, s)) for t in range(GROUPS) for s in range(PLACES)]


def ring_target(t, s):
    h, z, c = s // 16, s // 2 % 8, s % 2
    return flat(t, place_of(h, z + 1 - 2 * c, c))


FAR = pairs(lambda t, s: flat(t ^ 1, s ^ 16))
SWAP = pairs(lambda t, s: flat(t, s ^ 1))
RING = pairs(ring_target)
SAME_CORE = [[place_of(h, z, c) for h in range(2) for z in range(8)] for c in range(2)]
PEER_GROUPS = [
    [flat(t, place_of(h, z, c)) for t in range(GROUPS) for h in range(2)]
    for z in range(8)
    for c in range(2)
]


def index_kernel(term_order, connect, sector_at, sector_rows, front, mine, position):
    group, place = lax.axis_index("term"), lax.axis_index("sector")
    core = lax.rem(place, 2)
    half = lax.div(place, 16)
    z = lax.rem(lax.div(place, 2), 8)

    def put(p, carry):
        position[sector_at[p]] = p
        return carry

    lax.fori_loop(0, PLACES, put, 0)

    def note(k, carry):
        source = connect[sector_at[place], term_order[group * SLOTS + k]]
        p = position[source]
        step = lax.rem(lax.div(p, 2), 8) - z
        step = lax.rem(jnp.where(core == 0, -step, step) + 8, 8)
        side = jnp.where(lax.div(p, 16) == half, 0, 1)
        parity = jnp.where(lax.rem(p, 2) == core, 0, 1)
        mine[0, k] = step * 2 + parity
        mine[1, k] = side
        mine[2, k] = sector_rows[source]
        mine[3, k] = sector_rows[sector_at[place]]
        return carry

    lax.fori_loop(0, SLOTS, note, 0)

    def peer(m, carry):
        their_group = lax.div(m, 2)
        target = sector_at[lax.rem(m, 2) * 16 + lax.rem(place, 16)]

        def slot(k, carry):
            p = position[connect[target, term_order[their_group * SLOTS + k]]]
            front[m * SLOTS + k] = lax.div(p, 2) + jnp.where(lax.rem(p, 2) == core, 0, 16)
            return carry

        return lax.fori_loop(0, SLOTS, slot, carry)

    lax.fori_loop(0, PEERS, peer, 0)


def prepare_kernel(first, psi, copies, part, pieces, sem):
    start = pl.multiple_of(first[0], 2 * PART)
    near = pltpu.make_async_copy(psi.at[pl.ds(start, 2 * PART)], pieces, sem.at[0])
    rest = pltpu.make_async_copy(psi.at[pl.ds(FRONT, REST)], part, sem.at[1])
    near.start()
    rest.start()
    near.wait()
    for h in range(2):
        for z in range(PEERS // 2):
            copies[h * (PEERS // 2) + z] = pieces[h * PART : (h + 1) * PART]
    rest.wait()


def select_kernel(front, own, other, out, both, held, sem):
    both[:16] = own[...]
    both[16:] = other[...]

    def peer(m, carry):
        for k in range(SLOTS):
            held[m, k] = both[front[m * SLOTS + k]]
        pltpu.make_async_copy(held.at[m], out.at[m], sem).start()
        return carry

    lax.fori_loop(0, PEERS, peer, 0)
    pltpu.make_async_copy(held, out, sem).wait()


def product_kernel(mine, front, left, right, *refs):
    blocks, refs = refs[:PEERS], refs[PEERS:]
    out, fronts, rests, lefts, rights, block, acc, front_sem, rest_sem, left_sem, right_sem = refs

    def fetch_rest(j, low, high):
        if high - low == 1:
            ref = blocks[low]
            pltpu.make_async_copy(ref.at[mine[1, j]], rests.at[j], rest_sem.at[j]).start()
            return
        middle = (low + high) // 2
        below = mine[0, j] < middle

        @pl.when(below)
        def _():
            fetch_rest(j, low, middle)

        @pl.when(jnp.logical_not(below))
        def _():
            fetch_rest(j, middle, high)

    def fetch(j, carry):
        pltpu.make_async_copy(right.at[j], rights.at[j], right_sem.at[j]).start()
        pltpu.make_async_copy(front.at[:, j], fronts.at[j], front_sem.at[j]).start()
        fetch_rest(j, 0, PEERS)
        pltpu.make_async_copy(left.at[j, 0], lefts.at[j], left_sem.at[j]).start()
        return carry

    lax.fori_loop(0, SLOTS, fetch, 0)

    def arrived(buffer, sem, k):
        pltpu.make_async_copy(buffer.at[k], buffer.at[k], sem.at[k]).wait()

    def dot(a, b):
        return jnp.dot(a, b, preferred_element_type=jnp.float32)

    rows = lax.broadcasted_iota(jnp.int32, (BLK, BLK), 0)

    def wait(k):
        arrived(fronts, front_sem, k)
        arrived(rests, rest_sem, k)
        arrived(rights, right_sem, k)
        arrived(lefts, left_sem, k)

    def first_product(k):
        block[k % 2, :FRONT] = fronts[k].reshape(FRONT, BLK)
        block[k % 2, FRONT:] = rests[k]
        t = dot(block[k % 2], rights[k])
        t = jnp.where(rows < mine[2, k], t, 0.0)
        hi = t.astype(jnp.bfloat16)
        return hi, (t - hi.astype(jnp.float32)).astype(jnp.bfloat16)

    wait(0)
    following = first_product(0)
    for k in range(SLOTS):
        hi, lo = following
        if k + 1 < SLOTS:
            wait(k + 1)
            following = first_product(k + 1)
        part = dot(lefts[k], hi) + dot(lefts[k], lo)
        if k == 0:
            acc[...] = part
        else:
            acc[...] += part
    total = jnp.where(rows < mine[3, 0], acc[...], 0.0).T
    for g in range(GROUPS):
        piece = total[g * WIDTH : (g + 1) * WIDTH]
        largest = jnp.maximum(jnp.max(jnp.abs(piece), axis=0, keepdims=True), 1e-30)
        level = jnp.ceil(jnp.log(largest) * (LEVELS / LN2)) + 1.0
        steps = piece * (STEPS * jnp.exp(level * (-LN2 / LEVELS)))
        out[g, :WIDTH] = jnp.round(steps).astype(jnp.int32).astype(jnp.int16)
        out[g, WIDTH:] = jnp.broadcast_to(level, (16, BLK)).astype(jnp.int32).astype(jnp.int16)


def on_device(psi, left_blocks, right_ops, sector_rows, connect, term_order, sector_at):
    group = lax.axis_index("term")
    smem = pl.BlockSpec(memory_space=pltpu.SMEM)
    vmem = pl.BlockSpec(memory_space=pltpu.VMEM)
    anywhere = pl.BlockSpec(memory_space=pl.ANY)
    params = pltpu.CompilerParams(vmem_limit_bytes=VMEM_LIMIT)
    psi = psi[0]

    def hop(x, perm):
        return lax.ppermute(x, BOTH, perm)

    front_index, mine = pl.pallas_call(
        index_kernel,
        out_shape=(
            jax.ShapeDtypeStruct((PEERS * SLOTS,), jnp.int32),
            jax.ShapeDtypeStruct((4, SLOTS), jnp.int32),
        ),
        in_specs=[smem] * 4,
        out_specs=(smem, smem),
        scratch_shapes=[pltpu.SMEM((PLACES,), jnp.int32)],
        cost_estimate=pl.CostEstimate(flops=0, bytes_accessed=8 * 1024 * 1024, transcendentals=0),
    )(term_order, connect.T, sector_at, sector_rows)

    def after(x, y):
        return lax.optimization_barrier((x, y))[0]

    copies, part = pl.pallas_call(
        prepare_kernel,
        out_shape=(
            jax.ShapeDtypeStruct((PEERS, PART, BLK), psi.dtype),
            jax.ShapeDtypeStruct((REST, BLK), psi.dtype),
        ),
        in_specs=[smem, anywhere],
        out_specs=(vmem, vmem),
        scratch_shapes=[
            pltpu.VMEM((2 * PART, BLK), psi.dtype),
            pltpu.SemaphoreType.DMA((2,)),
        ],
        compiler_params=params,
    )(
        (group * 2 * PART).astype(jnp.int32)[None],
        pltpu.with_memory_space_constraint(psi, pltpu.HBM),
    )
    x = [jnp.stack([part, hop(part, FAR)])]
    y = [hop(x[0], SWAP)]
    own = lax.all_to_all(copies, "sector", 0, 0, axis_index_groups=SAME_CORE, tiled=True)
    own = after(own, front_index)
    other = hop(own, SWAP)
    chosen = pl.pallas_call(
        select_kernel,
        out_shape=pltpu.HBM((PEERS, SLOTS, PART, BLK), psi.dtype),
        in_specs=[smem] + [vmem] * 2,
        out_specs=anywhere,
        scratch_shapes=[
            pltpu.VMEM((PLACES, PART, BLK), psi.dtype),
            pltpu.VMEM((PEERS, SLOTS, PART, BLK), psi.dtype),
            pltpu.SemaphoreType.DMA,
        ],
        cost_estimate=pl.CostEstimate(flops=0, bytes_accessed=8 * 1024 * 1024, transcendentals=0),
        compiler_params=params,
    )(pltpu.with_memory_space_constraint(front_index, pltpu.HBM), own, other)
    front = lax.all_to_all(chosen, BOTH, 0, 0, axis_index_groups=PEER_GROUPS, tiled=True)
    for step in range(1, 5):
        x.append(hop(x[-1], RING))
        if step < 4:
            y.append(hop(y[-1], RING))
    x_swapped = [None] + [hop(v, SWAP) for v in x[1:]]
    y_swapped = [None] + [hop(v, SWAP) for v in y[1:]]
    blocks = []
    for step in range(4):
        blocks += [x[step], y[step]]
    blocks += [x[4], x_swapped[4]]
    for step in (3, 2, 1):
        blocks += [y_swapped[step], x_swapped[step]]

    summed = pl.pallas_call(
        product_kernel,
        out_shape=jax.ShapeDtypeStruct((GROUPS, WIDTH + 16, BLK), jnp.int16),
        in_specs=[smem] + [anywhere] * (3 + PEERS),
        out_specs=vmem,
        scratch_shapes=[
            pltpu.VMEM((SLOTS, PEERS, PART, BLK), jnp.bfloat16),
            pltpu.VMEM((SLOTS, REST, BLK), jnp.bfloat16),
            pltpu.VMEM((SLOTS, BLK, BLK), jnp.bfloat16),
            pltpu.VMEM((SLOTS, BLK, BLK), jnp.bfloat16),
            pltpu.VMEM((2, BLK, BLK), jnp.bfloat16),
            pltpu.VMEM((BLK, BLK), jnp.float32),
        ]
        + [pltpu.SemaphoreType.DMA((SLOTS,))] * 4,
        compiler_params=params,
    )(
        mine,
        front,
        left_blocks,
        right_ops,
        *[pltpu.with_memory_space_constraint(b, pltpu.HBM) for b in blocks],
    )
    parts = lax.all_to_all(summed, "term", 0, 0, tiled=True).astype(jnp.float32)
    sizes = jnp.exp(parts[:, WIDTH:WIDTH + 1] * (LN2 / LEVELS)) * (1.0 / STEPS)
    return jnp.sum(parts[:, :WIDTH] * sizes, axis=0).T[None]


def solution(mesh):
    placed = (
        P("sector", None, None),
        P("term", "sector", None, None),
        P("term", None, None),
        P(),
        P(),
        P(),
        P(),
    )
    return jax.shard_map(
        on_device, mesh=mesh, in_specs=placed, out_specs=P("sector", None, "term"), check_vma=False
    )
```

```python
import functools

import jax
import jax.numpy as jnp
from jax import lax
from jax.experimental import pallas as pl
from jax.experimental.pallas import tpu as pltpu
from jax.sharding import PartitionSpec as P

GROUPS = 8
SLOTS = 8
PLACES = 32
BLK = 512
PEERS = 16
FRONT = 256
REST = BLK - FRONT
PART = FRONT // PEERS
BOTH = ("term", "sector")
LN2 = 0.6931471805599453
LEVELS = 64.0
STEPS = 32766.0
WIDTH = BLK // GROUPS
VMEM_LIMIT = 48 * 1024 * 1024


def flat(t, s):
    return t * PLACES + s


def place_of(h, z, c):
    return (h * 8 + z % 8) * 2 + c


def pairs(f):
    return [(flat(t, s), f(t, s)) for t in range(GROUPS) for s in range(PLACES)]


def ring_target(t, s):
    h, z, c = s // 16, s // 2 % 8, s % 2
    return flat(t, place_of(h, z + 1 - 2 * c, c))


FAR = pairs(lambda t, s: flat(t ^ 1, s ^ 16))
SWAP = pairs(lambda t, s: flat(t, s ^ 1))
RING = pairs(ring_target)
SAME_CORE = [[place_of(h, z, c) for h in range(2) for z in range(8)] for c in range(2)]
PEER_GROUPS = [
    [flat(t, place_of(h, z, c)) for t in range(GROUPS) for h in range(2)]
    for z in range(8)
    for c in range(2)
]


def index_kernel(term_order, connect, sector_at, sector_rows, front, mine, position):
    group, place = lax.axis_index("term"), lax.axis_index("sector")
    core = lax.rem(place, 2)
    half = lax.div(place, 16)
    z = lax.rem(lax.div(place, 2), 8)

    def put(p, carry):
        position[sector_at[p]] = p
        return carry

    lax.fori_loop(0, PLACES, put, 0)

    def note(k, carry):
        source = connect[sector_at[place], term_order[group * SLOTS + k]]
        p = position[source]
        step = lax.rem(lax.div(p, 2), 8) - z
        step = lax.rem(jnp.where(core == 0, -step, step) + 8, 8)
        side = jnp.where(lax.div(p, 16) == half, 0, 1)
        parity = jnp.where(lax.rem(p, 2) == core, 0, 1)
        mine[0, k] = step * 2 + parity
        mine[1, k] = side
        mine[2, k] = sector_rows[source]
        mine[3, k] = sector_rows[sector_at[place]]
        return carry

    lax.fori_loop(0, SLOTS, note, 0)

    def peer(m, carry):
        their_group = lax.div(m, 2)
        target = sector_at[lax.rem(m, 2) * 16 + lax.rem(place, 16)]

        def slot(k, carry):
            p = position[connect[target, term_order[their_group * SLOTS + k]]]
            front[m * SLOTS + k] = lax.div(p, 2) + jnp.where(lax.rem(p, 2) == core, 0, 16)
            return carry

        return lax.fori_loop(0, SLOTS, slot, carry)

    lax.fori_loop(0, PEERS, peer, 0)


def prepare_kernel(first, psi, copies, part, pieces, sem):
    start = pl.multiple_of(first[0], 2 * PART)
    near = pltpu.make_async_copy(psi.at[pl.ds(start, 2 * PART)], pieces, sem.at[0])
    rest = pltpu.make_async_copy(psi.at[pl.ds(FRONT, REST)], part, sem.at[1])
    near.start()
    rest.start()
    near.wait()
    for h in range(2):
        for z in range(PEERS // 2):
            spread = pltpu.make_async_copy(
                pieces.at[pl.ds(h * PART, PART)], copies.at[h * (PEERS // 2) + z], sem.at[2]
            )
            spread.start()
    pltpu.make_async_copy(copies, copies, sem.at[2]).wait()
    rest.wait()


def select_kernel(front, own, other, out, both, held, sem):
    both[:16] = own[...]
    both[16:] = other[...]

    def peer(m, carry):
        for k in range(SLOTS):
            held[m, k] = both[front[m * SLOTS + k]]
        pltpu.make_async_copy(held.at[m], out.at[m], sem).start()
        return carry

    lax.fori_loop(0, PEERS, peer, 0)
    pltpu.make_async_copy(held, out, sem).wait()


def product_kernel(mine, front, left, right, *refs):
    blocks, refs = refs[:PEERS], refs[PEERS:]
    out, fronts, rests, lefts, rights, block, acc, front_sem, rest_sem, left_sem, right_sem = refs

    def fetch_rest(j, low, high):
        if high - low == 1:
            ref = blocks[low]
            pltpu.make_async_copy(ref.at[mine[1, j]], rests.at[j], rest_sem.at[j]).start()
            return
        middle = (low + high) // 2
        below = mine[0, j] < middle

        @pl.when(below)
        def _():
            fetch_rest(j, low, middle)

        @pl.when(jnp.logical_not(below))
        def _():
            fetch_rest(j, middle, high)

    def fetch(j, carry):
        pltpu.make_async_copy(right.at[j], rights.at[j], right_sem.at[j]).start()
        pltpu.make_async_copy(front.at[:, j], fronts.at[j], front_sem.at[j]).start()
        fetch_rest(j, 0, PEERS)
        pltpu.make_async_copy(left.at[j, 0], lefts.at[j], left_sem.at[j]).start()
        return carry

    lax.fori_loop(0, SLOTS, fetch, 0)

    def arrived(buffer, sem, k):
        pltpu.make_async_copy(buffer.at[k], buffer.at[k], sem.at[k]).wait()

    def dot(a, b):
        return jnp.dot(a, b, preferred_element_type=jnp.float32)

    rows = lax.broadcasted_iota(jnp.int32, (BLK, BLK), 0)

    def wait(k):
        arrived(fronts, front_sem, k)
        arrived(rests, rest_sem, k)
        arrived(rights, right_sem, k)
        arrived(lefts, left_sem, k)

    def first_product(k):
        block[k % 2, :FRONT] = fronts[k].reshape(FRONT, BLK)
        block[k % 2, FRONT:] = rests[k]
        t = dot(block[k % 2], rights[k])
        t = jnp.where(rows < mine[2, k], t, 0.0)
        hi = t.astype(jnp.bfloat16)
        return hi, (t - hi.astype(jnp.float32)).astype(jnp.bfloat16)

    wait(0)
    following = first_product(0)
    for k in range(SLOTS):
        hi, lo = following
        if k + 1 < SLOTS:
            wait(k + 1)
            following = first_product(k + 1)
        part = dot(lefts[k], hi) + dot(lefts[k], lo)
        if k == 0:
            acc[...] = part
        else:
            acc[...] += part
    total = jnp.where(rows < mine[3, 0], acc[...], 0.0).T
    for g in range(GROUPS):
        piece = total[g * WIDTH : (g + 1) * WIDTH]
        largest = jnp.maximum(jnp.max(jnp.abs(piece), axis=0, keepdims=True), 1e-30)
        level = jnp.ceil(jnp.log(largest) * (LEVELS / LN2)) + 1.0
        steps = piece * (STEPS * jnp.exp(level * (-LN2 / LEVELS)))
        out[g % 2 * 4 + g // 2, :WIDTH] = jnp.round(steps).astype(jnp.int32).astype(jnp.int16)
        out[g % 2 * 4 + g // 2, WIDTH:] = jnp.broadcast_to(level, (16, BLK)).astype(jnp.int32).astype(jnp.int16)


def on_device(psi, left_blocks, right_ops, sector_rows, connect, term_order, sector_at):
    group = lax.axis_index("term")
    smem = pl.BlockSpec(memory_space=pltpu.SMEM)
    vmem = pl.BlockSpec(memory_space=pltpu.VMEM)
    anywhere = pl.BlockSpec(memory_space=pl.ANY)
    params = pltpu.CompilerParams(vmem_limit_bytes=VMEM_LIMIT)
    psi = psi[0]

    def hop(x, perm):
        return lax.ppermute(x, BOTH, perm)

    front_index, mine = pl.pallas_call(
        index_kernel,
        out_shape=(
            jax.ShapeDtypeStruct((PEERS * SLOTS,), jnp.int32),
            jax.ShapeDtypeStruct((4, SLOTS), jnp.int32),
        ),
        in_specs=[smem] * 4,
        out_specs=(smem, smem),
        scratch_shapes=[pltpu.SMEM((PLACES,), jnp.int32)],
        cost_estimate=pl.CostEstimate(flops=0, bytes_accessed=8 * 1024 * 1024, transcendentals=0),
    )(term_order, connect.T, sector_at, sector_rows)

    def after(x, y):
        return lax.optimization_barrier((x, y))[0]

    copies, part = pl.pallas_call(
        prepare_kernel,
        out_shape=(
            pltpu.HBM((PEERS, PART, BLK), psi.dtype),
            jax.ShapeDtypeStruct((REST, BLK), psi.dtype),
        ),
        in_specs=[smem, anywhere],
        out_specs=(anywhere, vmem),
        scratch_shapes=[
            pltpu.VMEM((2 * PART, BLK), psi.dtype),
            pltpu.SemaphoreType.DMA((3,)),
        ],
        compiler_params=params,
    )(
        (group * 2 * PART).astype(jnp.int32)[None],
        pltpu.with_memory_space_constraint(psi, pltpu.HBM),
    )
    x = [jnp.stack([part, hop(part, FAR)])]
    y = [hop(x[0], SWAP)]
    own = lax.all_to_all(copies, "sector", 0, 0, axis_index_groups=SAME_CORE, tiled=True)
    own = after(own, front_index)
    other = hop(own, SWAP)
    chosen = pl.pallas_call(
        select_kernel,
        out_shape=pltpu.HBM((PEERS, SLOTS, PART, BLK), psi.dtype),
        in_specs=[smem] + [vmem] * 2,
        out_specs=anywhere,
        scratch_shapes=[
            pltpu.VMEM((PLACES, PART, BLK), psi.dtype),
            pltpu.VMEM((PEERS, SLOTS, PART, BLK), psi.dtype),
            pltpu.SemaphoreType.DMA,
        ],
        cost_estimate=pl.CostEstimate(flops=0, bytes_accessed=8 * 1024 * 1024, transcendentals=0),
        compiler_params=params,
    )(pltpu.with_memory_space_constraint(front_index, pltpu.HBM), own, other)
    front = lax.all_to_all(chosen, BOTH, 0, 0, axis_index_groups=PEER_GROUPS, tiled=True)
    for step in range(1, 5):
        x.append(hop(x[-1], RING))
        if step < 4:
            y.append(hop(y[-1], RING))
    x_swapped = [None] + [hop(v, SWAP) for v in x[1:]]
    y_swapped = [None] + [hop(v, SWAP) for v in y[1:]]
    blocks = []
    for step in range(4):
        blocks += [x[step], y[step]]
    blocks += [x[4], x_swapped[4]]
    for step in (3, 2, 1):
        blocks += [y_swapped[step], x_swapped[step]]

    summed = pl.pallas_call(
        product_kernel,
        out_shape=jax.ShapeDtypeStruct((GROUPS, WIDTH + 16, BLK), jnp.int16),
        in_specs=[smem] + [anywhere] * (3 + PEERS),
        out_specs=vmem,
        scratch_shapes=[
            pltpu.VMEM((SLOTS, PEERS, PART, BLK), jnp.bfloat16),
            pltpu.VMEM((SLOTS, REST, BLK), jnp.bfloat16),
            pltpu.VMEM((SLOTS, BLK, BLK), jnp.bfloat16),
            pltpu.VMEM((SLOTS, BLK, BLK), jnp.bfloat16),
            pltpu.VMEM((2, BLK, BLK), jnp.bfloat16),
            pltpu.VMEM((BLK, BLK), jnp.float32),
        ]
        + [pltpu.SemaphoreType.DMA((SLOTS,))] * 4,
        compiler_params=params,
    )(
        mine,
        front,
        left_blocks,
        right_ops,
        *[pltpu.with_memory_space_constraint(b, pltpu.HBM) for b in blocks],
    )
    parts = lax.all_to_all(
        summed, "term", 0, 0, axis_index_groups=[[y * 2 + x for x in range(2) for y in range(4)]], tiled=True
    ).astype(jnp.float32)
    sizes = jnp.exp(parts[:, WIDTH:WIDTH + 1] * (LN2 / LEVELS)) * (1.0 / STEPS)
    return jnp.sum(parts[:, :WIDTH] * sizes, axis=0).T[None]


def solution(mesh):
    placed = (
        P("sector", None, None),
        P("term", "sector", None, None),
        P("term", None, None),
        P(),
        P(),
        P(),
        P(),
    )
    return jax.shard_map(
        on_device, mesh=mesh, in_specs=placed, out_specs=P("sector", None, "term"), check_vma=False
    )
```
